32 devices in a mesh: frame: 4 (over y, core), patch: 8 (over z, x).
Axes of the slice: x: 2, y: 2, z: 4, core: 2. Of those that a mesh axis runs over, the one named last changes fastest.
Arguments:
- q_space: bfloat16 [32, 8, 512, 128], P('frame', None, 'patch'), may hold values from -8 to 8
- k_space: bfloat16 [32, 8, 512, 128], P('frame', None, 'patch'), may hold values from -8 to 8
- v_space: bfloat16 [32, 8, 512, 128], P('frame', None, 'patch'), may hold values from -6 to 6
- d_out_space: bfloat16 [32, 8, 512, 128], P('frame', None, 'patch'), may hold values from -6 to 6
- q_time: bfloat16 [32, 8, 512, 128], P('frame', None, 'patch'), may hold values from -8 to 8
- k_time: bfloat16 [32, 8, 512, 128], P('frame', None, 'patch'), may hold values from -8 to 8
- v_time: bfloat16 [32, 8, 512, 128], P('frame', None, 'patch'), may hold values from -6 to 6
- d_out_time: bfloat16 [32, 8, 512, 128], P('frame', None, 'patch'), may hold values from -6 to 6
Outputs:
- grad_q_space: bfloat16 [32, 8, 512, 128], P('frame', None, 'patch')
- grad_k_space: bfloat16 [32, 8, 512, 128], P('frame', None, 'patch')
- grad_v_space: bfloat16 [32, 8, 512, 128], P('frame', None, 'patch')
- grad_q_time: bfloat16 [32, 8, 512, 128], P('frame', None, 'patch')
- grad_k_time: bfloat16 [32, 8, 512, 128], P('frame', None, 'patch')
- grad_v_time: bfloat16 [32, 8, 512, 128], P('frame', None, 'patch')
The draws below stay inside these ranges and needn't reach their ends.
All inputs are finite; a program needn't handle non-finite values.
Results may differ from the reference program's by a relative error of at most 0.0071.
Values may be sent and summed in bfloat16 or wider, within the bound.
A program may use at most 128 MiB of HBM per device.

```python
import math
import jax
import jax.numpy as jnp
from jax import lax

HEADS = 8
HEAD_DIM = 128
FRAMES = 32
PATCHES = 512


def pair_draw(key, salt_value, item_shape, length, width):
    key = jax.random.fold_in(key, salt_value)
    subkeys = jax.random.split(key, 3)
    full_shape = item_shape + (length, width)
    query_rows = jnp.clip(jax.random.normal(subkeys[0], full_shape, jnp.float32), -6.0, 6.0)
    key_rows = jnp.clip(jax.random.normal(subkeys[2], full_shape, jnp.float32), -6.0, 6.0)
    return (query_rows, key_rows)


def draw_q_space(key, part):
    return pair_draw(key, 11, (FRAMES, HEADS), PATCHES, HEAD_DIM)[0].astype(jnp.bfloat16)


def draw_k_space(key, part):
    return pair_draw(key, 11, (FRAMES, HEADS), PATCHES, HEAD_DIM)[1].astype(jnp.bfloat16)


def draw_q_time(key, part):
    return jnp.transpose(pair_draw(key, 23, (HEADS, PATCHES), FRAMES, HEAD_DIM)[0], (2, 0, 1, 3)).astype(jnp.bfloat16)


def draw_k_time(key, part):
    return jnp.transpose(pair_draw(key, 23, (HEADS, PATCHES), FRAMES, HEAD_DIM)[1], (2, 0, 1, 3)).astype(jnp.bfloat16)


def steps_of(rng, extent, pieces, least, high):
    def one(dim, shards_of):
        heights = jax.random.uniform(jax.random.fold_in(jax.random.fold_in(rng, 6), dim), (shards_of,), jnp.float32, least / len(pieces), high / len(pieces))
        return jnp.repeat(jnp.exp(heights), extent[dim] // shards_of).reshape((-1,) + (1,) * (len(extent) - dim - 1))

    level = one(*pieces[0])
    for cut in pieces[1:]:
        level = level * one(*cut)
    return level


def scatter_about(stream_key, shape, deviation, reach, cuts=(), kind=jnp.bfloat16):
    loudness = steps_of(stream_key, shape, cuts, -0.22, 0.18) if cuts else 1.0
    values = jax.random.normal(stream_key, shape, jnp.float32) * deviation * loudness
    return jnp.minimum(jnp.maximum(values, -reach), reach).astype(kind)


def setup_inputs(seed: int = 0) -> dict:
    splits = jax.random.split(jax.random.key(seed), 9)
    return {
        "q_space": draw_q_space(jax.random.fold_in(splits[8], 71), 0),
        "k_space": draw_k_space(jax.random.fold_in(splits[8], 71), 0),
        "v_space": scatter_about(splits[2], (FRAMES, HEADS, PATCHES, HEAD_DIM), 1.0, 6.0, ((0, 4), (2, 8))),
        "d_out_space": scatter_about(splits[3], (FRAMES, HEADS, PATCHES, HEAD_DIM), 1.0, 6.0, ((0, 4), (2, 8))),
        "q_time": draw_q_time(jax.random.fold_in(splits[8], 71), 0),
        "k_time": draw_k_time(jax.random.fold_in(splits[8], 71), 0),
        "v_time": scatter_about(splits[6], (FRAMES, HEADS, PATCHES, HEAD_DIM), 1.0, 6.0, ((0, 4), (2, 8))),
        "d_out_time": scatter_about(splits[7], (FRAMES, HEADS, PATCHES, HEAD_DIM), 1.0, 6.0, ((0, 4), (2, 8))),
    }


def attention_grads(queries, key_rows, values, out_grad, causal):
    inverse_root_scale = 1.0 / math.sqrt(queries.shape[-1])
    query_wide = queries.astype(jnp.float32)
    key_wide = key_rows.astype(jnp.float32)
    value_wide = values.astype(jnp.float32)
    gradient_upstream = out_grad.astype(jnp.float32)
    score_logits = jnp.einsum('uej,uoj->ueo', query_wide, key_wide) * inverse_root_scale
    if causal:
        length = score_logits.shape[-1]
        allowed = jnp.arange(length)[:, None] >= jnp.arange(length)[None, :]
        score_logits = jnp.where(allowed, score_logits, -1e+30)
    row_max = lax.optimization_barrier(jnp.max(score_logits, axis=-1, keepdims=True))
    raised = jnp.exp(score_logits - row_max)
    softmax_rows = raised / lax.optimization_barrier(jnp.sum(raised, axis=-1, keepdims=True))
    weight_probabilities = lax.optimization_barrier(softmax_rows.astype(jnp.bfloat16)).astype(jnp.float32)
    output_tensor = jnp.einsum('jgf,jfi->jgi', weight_probabilities, value_wide)
    delta_rows = lax.optimization_barrier(jnp.sum(gradient_upstream * output_tensor, axis=-1))
    value_gradient = jnp.einsum('euw,euh->ewh', weight_probabilities, gradient_upstream).astype(jnp.bfloat16)
    probability_gradient = jnp.einsum('uej,uoj->ueo', gradient_upstream, value_wide)
    logit_gradient = softmax_rows * (probability_gradient - delta_rows[..., None])
    logit_gradient = lax.optimization_barrier(logit_gradient.astype(jnp.bfloat16)).astype(jnp.float32)
    query_gradient = (jnp.einsum('jgf,jfi->jgi', logit_gradient, key_wide) * inverse_root_scale).astype(jnp.bfloat16)
    key_gradient = (jnp.einsum('euw,euh->ewh', logit_gradient, query_wide) * inverse_root_scale).astype(jnp.bfloat16)
    return (query_gradient, key_gradient, value_gradient)

def space_frame(parts):
    return attention_grads(parts[0], parts[1], parts[2], parts[3], False)

def time_head(parts):
    return attention_grads(parts[0], parts[1], parts[2], parts[3], True)

def reference(q_space, k_space, v_space, d_out_space, q_time, k_time, v_time, d_out_time):
    space_q, space_k, space_v = lax.map(space_frame, (q_space, k_space, v_space, d_out_space))
    moved = tuple((jnp.transpose(block, (1, 2, 0, 3)) for block in (q_time, k_time, v_time, d_out_time)))
    time_q, time_k, time_v = lax.map(time_head, moved)
    time_q = jnp.transpose(time_q, (2, 0, 1, 3))
    time_k = jnp.transpose(time_k, (2, 0, 1, 3))
    time_v = jnp.transpose(time_v, (2, 0, 1, 3))
    return (space_q, space_k, space_v, time_q, time_k, time_v)
```

```python
import functools
import math

import jax
import jax.numpy as jnp
from jax import lax
from jax.experimental import pallas as pl
from jax.experimental.pallas import tpu as pltpu
from jax.sharding import PartitionSpec as P

MESH = pl.DeviceIdType.MESH
ROWS = 16
BLOCK = 256


def flip_dot(left, right):
    return lax.dot_general(
        left, right, (((1,), (1,)), ((), ())), preferred_element_type=jnp.float32
    )


def lead_dot(left, right):
    return lax.dot_general(
        left, right, (((0,), (0,)), ((), ())), preferred_element_type=jnp.float32
    )


def attend(length, scale, group, load, store, dk_acc, dv_acc):
    for start in range(0, length, BLOCK):
        rows = min(BLOCK, length - start)
        seen = start + rows if group else length
        query = load(0, start, rows)
        keys = load(1, 0, seen)
        values = load(2, 0, seen)
        upstream = load(3, start, rows)
        scores = flip_dot(keys, query) * scale
        if group:
            gap = (
                lax.broadcasted_iota(jnp.int32, (seen, rows), 1)
                + start
                - lax.broadcasted_iota(jnp.int32, (seen, rows), 0)
            )
            allowed = jnp.logical_and(gap >= 0, (gap & (group - 1)) == 0)
            scores = jnp.where(allowed, scores, -1e30)
        raised = jnp.exp(scores - jnp.max(scores, axis=0, keepdims=True))
        soft = raised * (1.0 / jnp.sum(raised, axis=0, keepdims=True))
        weights = soft.astype(jnp.bfloat16)
        grad_prob = flip_dot(values, upstream)
        delta = jnp.sum(weights.astype(jnp.float32) * grad_prob, axis=0, keepdims=True)
        grad_score = (soft * (grad_prob - delta)).astype(jnp.bfloat16)
        dv = jnp.dot(weights, upstream, preferred_element_type=jnp.float32)
        dk = jnp.dot(grad_score, query, preferred_element_type=jnp.float32)
        store(0, start, (lead_dot(grad_score, keys) * scale).astype(jnp.bfloat16))
        if start == 0 and seen < length:
            dk_acc[pl.ds(seen, length - seen), :] = jnp.zeros((length - seen, dk.shape[1]), jnp.float32)
            dv_acc[pl.ds(seen, length - seen), :] = jnp.zeros((length - seen, dv.shape[1]), jnp.float32)
        if start == 0:
            dk_acc[pl.ds(0, seen), :] = dk
            dv_acc[pl.ds(0, seen), :] = dv
        else:
            dk_acc[pl.ds(0, seen), :] += dk
            dv_acc[pl.ds(0, seen), :] += dv
    store(1, 0, (dk_acc[pl.ds(0, length), :] * scale).astype(jnp.bfloat16))
    store(2, 0, dv_acc[pl.ds(0, length), :].astype(jnp.bfloat16))


def kernel(plan, *refs):
    space_in, time_in = refs[0:4], refs[4:8]
    space_out, time_out = refs[8:11], refs[11:14]
    (sp, sp_res, tm, tm_res, dk_acc, dv_acc) = refs[14:20]
    (sp_recv, sp_send, spb_recv, spb_send, tm_recv, tm_send, tmb_recv, tmb_send) = refs[20:]
    n_patch, n_frame, per_dev, rows, frames, heads_dev, span, scale = plan
    length = n_patch * rows
    me_p = lax.axis_index("patch")
    me_f = lax.axis_index("frame")

    def patch_peer(step):
        return lax.rem(me_p + step, n_patch)

    def frame_peer(step):
        return lax.rem(me_f + step, n_frame)

    def time_slot(owner):
        if span == rows:
            return pl.ds(owner * heads_dev, heads_dev), pl.ds(0, span)
        cuts = rows // span
        return (
            pl.ds(owner // cuts, 1),
            pl.ds(pl.multiple_of(lax.rem(owner, cuts) * span, span), span),
        )

    barrier = pltpu.get_barrier_semaphore()
    for step in range(1, n_patch):
        pl.semaphore_signal(barrier, inc=1, device_id={"patch": patch_peer(step)}, device_id_type=MESH)
    for step in range(1, n_frame):
        pl.semaphore_signal(barrier, inc=1, device_id={"frame": frame_peer(step)}, device_id_type=MESH)
    pl.semaphore_wait(barrier, n_patch + n_frame - 2)

    my_rows = pl.ds(pl.multiple_of(me_p * rows, rows), rows)
    pieces = max(1, per_dev // 2)
    piece_frames = frames // pieces

    def send_space(c):
        for step in range(1, n_patch):
            peer = patch_peer(step)
            for a in range(4):
                pltpu.make_async_remote_copy(
                    src_ref=space_in[a].at[peer * per_dev + c],
                    dst_ref=sp.at[c, a, my_rows],
                    send_sem=sp_send.at[c],
                    recv_sem=sp_recv.at[c],
                    device_id={"patch": peer},
                    device_id_type=MESH,
                ).start()
        for a in range(4):
            pltpu.make_async_copy(
                space_in[a].at[me_p * per_dev + c], sp.at[c, a, my_rows], sp_recv.at[c]
            ).start()

    def send_time(c):
        here = pl.ds(c * piece_frames, piece_frames)
        there = pl.ds(me_f * frames + c * piece_frames, piece_frames)
        for step in range(1, n_frame):
            peer = frame_peer(step)
            hs, ps = time_slot(peer)
            for a in range(4):
                pltpu.make_async_remote_copy(
                    src_ref=time_in[a].at[here, hs, ps],
                    dst_ref=tm.at[a, there],
                    send_sem=tm_send.at[0],
                    recv_sem=tm_recv.at[0],
                    device_id={"frame": peer},
                    device_id_type=MESH,
                ).start()
        hs, ps = time_slot(me_f)
        for a in range(4):
            pltpu.make_async_copy(time_in[a].at[here, hs, ps], tm.at[a, there], tm_recv.at[0]).start()

    @pl.loop(0, pieces)
    def _(c):
        send_space(c)
        send_time(c)

    @pl.loop(pieces, per_dev)
    def _(c):
        send_space(c)

    def all_time():
        pltpu.make_async_copy(tm, tm, tm_recv.at[0]).wait()
        units = span // ROWS
        total = n_frame * frames

        @pl.loop(0, heads_dev * units)
        def _(u):
            hh = u // units
            ps = pl.ds(pl.multiple_of(lax.rem(u, units) * ROWS, ROWS), ROWS)

            def load(a, start, count):
                block = tm[a, pl.ds(start // ROWS, count // ROWS), hh, ps, :]
                return block.reshape(count, block.shape[-1])

            def store(a, start, value):
                count = value.shape[0]
                tm_res[a, pl.ds(start // ROWS, count // ROWS), hh, ps, :] = value.reshape(
                    count // ROWS, ROWS, value.shape[1]
                )

            attend(total * ROWS, scale, ROWS, load, store, dk_acc, dv_acc)

        hs, ps = time_slot(me_f)
        for step in range(1, n_frame):
            peer = frame_peer(step)
            for a in range(3):
                pltpu.make_async_remote_copy(
                    src_ref=tm_res.at[a, pl.ds(peer * frames, frames)],
                    dst_ref=time_out[a].at[:, hs, ps],
                    send_sem=tmb_send.at[0],
                    recv_sem=tmb_recv.at[a],
                    device_id={"frame": peer},
                    device_id_type=MESH,
                ).start()
        for a in range(3):
            pltpu.make_async_copy(
                tm_res.at[a, pl.ds(me_f * frames, frames)], time_out[a].at[:, hs, ps], tmb_recv.at[a]
            ).start()

    @pl.loop(0, per_dev)
    def _(c):
        @pl.when(c == pieces)
        def _():
            all_time()

        pltpu.make_async_copy(sp.at[c], sp.at[c], sp_recv.at[c]).wait()

        def load(a, start, count):
            return sp[c, a, pl.ds(start, count), :]

        def store(a, start, value):
            sp_res[c, a, pl.ds(start, value.shape[0]), :] = value

        attend(length, scale, 0, load, store, dk_acc, dv_acc)
        seq = me_p * per_dev + c
        for step in range(1, n_patch):
            peer = patch_peer(step)
            for a in range(3):
                pltpu.make_async_remote_copy(
                    src_ref=sp_res.at[c, a, pl.ds(pl.multiple_of(peer * rows, rows), rows)],
                    dst_ref=space_out[a].at[seq],
                    send_sem=spb_send.at[c],
                    recv_sem=spb_recv.at[a],
                    device_id={"patch": peer},
                    device_id_type=MESH,
                ).start()
        for a in range(3):
            pltpu.make_async_copy(sp_res.at[c, a, my_rows], space_out[a].at[seq], spb_recv.at[a]).start()

    others = pl.ds(0, length - rows)
    away = pl.ds(0, (n_frame - 1) * frames)

    @pl.loop(0, per_dev)
    def _(c):
        pltpu.make_async_copy(sp.at[c, :, others], sp.at[c, :, others], sp_send.at[c]).wait()
        pltpu.make_async_copy(sp_res.at[c, :, others], sp_res.at[c, :, others], spb_send.at[c]).wait()

    pltpu.make_async_copy(tm.at[:, away], tm.at[:, away], tm_send.at[0]).wait()
    pltpu.make_async_copy(tm_res.at[:, away], tm_res.at[:, away], tmb_send.at[0]).wait()
    for a in range(3):
        pltpu.make_async_copy(time_out[a], time_out[a], tmb_recv.at[a]).wait()
        pltpu.make_async_copy(space_out[a], space_out[a], spb_recv.at[a]).wait()


def per_device(n_frame, n_patch, *blocks):
    frames, heads, rows, dim = blocks[0].shape
    per_dev = frames * heads // n_patch
    if n_frame <= heads:
        heads_dev, span = heads // n_frame, rows
    else:
        heads_dev, span = 1, rows * heads // n_frame
    length = n_patch * rows
    total = n_frame * frames
    scale = 1.0 / math.sqrt(dim)
    plan = (n_patch, n_frame, per_dev, rows, frames, heads_dev, span, scale)
    longest = max(length, total * ROWS)
    flat = (frames * heads, rows, dim)
    whole = (frames, heads, rows, dim)
    bf16 = jnp.bfloat16
    hbm = pl.BlockSpec(memory_space=pl.ANY)
    dma = pltpu.SemaphoreType.DMA
    outs = pl.pallas_call(
        functools.partial(kernel, plan),
        out_shape=[jax.ShapeDtypeStruct(flat, bf16)] * 3 + [jax.ShapeDtypeStruct(whole, bf16)] * 3,
        in_specs=[hbm] * 8,
        out_specs=[hbm] * 6,
        scratch_shapes=[
            pltpu.VMEM((per_dev, 4, length, dim), bf16),
            pltpu.VMEM((per_dev, 3, length, dim), bf16),
            pltpu.VMEM((4, total, heads_dev, span, dim), bf16),
            pltpu.VMEM((3, total, heads_dev, span, dim), bf16),
            pltpu.VMEM((longest, dim), jnp.float32),
            pltpu.VMEM((longest, dim), jnp.float32),
            dma((per_dev,)),
            dma((per_dev,)),
            dma((3,)),
            dma((per_dev,)),
            dma((1,)),
            dma((1,)),
            dma((3,)),
            dma((1,)),
        ],
        compiler_params=pltpu.CompilerParams(
            collective_id=0, has_side_effects=True, vmem_limit_bytes=56 * 1024 * 1024
        ),
    )(*[b.reshape(flat) for b in blocks[:4]], *blocks[4:])
    return tuple(o.reshape(whole) for o in outs)


def solution(mesh):
    spec = P("frame", None, "patch", None)
    return jax.shard_map(
        functools.partial(per_device, mesh.shape["frame"], mesh.shape["patch"]),
        mesh=mesh,
        in_specs=(spec,) * 8,
        out_specs=(spec,) * 6,
        check_vma=False,
    )
```

```python
import functools
import math

import jax
import jax.numpy as jnp
from jax import lax
from jax.experimental import pallas as pl
from jax.experimental.pallas import tpu as pltpu
from jax.sharding import PartitionSpec as P

MESH = pl.DeviceIdType.MESH
ROWS = 16
BLOCK = 256


def flip_dot(left, right):
    return lax.dot_general(
        left, right, (((1,), (1,)), ((), ())), preferred_element_type=jnp.float32
    )


def lead_dot(left, right):
    return lax.dot_general(
        left, right, (((0,), (0,)), ((), ())), preferred_element_type=jnp.float32
    )


def attend(length, scale, group, load, store, dk_acc, dv_acc):
    for start in range(0, length, BLOCK):
        rows = min(BLOCK, length - start)
        seen = start + rows if group else length
        query = load(0, start, rows)
        keys = load(1, 0, seen)
        values = load(2, 0, seen)
        upstream = load(3, start, rows)
        scores = flip_dot(keys, query) * scale
        if group:
            gap = (
                lax.broadcasted_iota(jnp.int32, (seen, rows), 1)
                + start
                - lax.broadcasted_iota(jnp.int32, (seen, rows), 0)
            )
            allowed = jnp.logical_and(gap >= 0, (gap & (group - 1)) == 0)
            scores = jnp.where(allowed, scores, -1e30)
        raised = jnp.exp(scores - jnp.max(scores, axis=0, keepdims=True))
        soft = raised * (1.0 / jnp.sum(raised, axis=0, keepdims=True))
        weights = soft.astype(jnp.bfloat16)
        grad_prob = flip_dot(values, upstream)
        delta = jnp.sum(weights.astype(jnp.float32) * grad_prob, axis=0, keepdims=True)
        grad_score = (soft * (grad_prob - delta)).astype(jnp.bfloat16)
        dv = jnp.dot(weights, upstream, preferred_element_type=jnp.float32)
        dk = jnp.dot(grad_score, query, preferred_element_type=jnp.float32)
        store(0, start, (lead_dot(grad_score, keys) * scale).astype(jnp.bfloat16))
        if start == 0 and seen < length:
            dk_acc[pl.ds(seen, length - seen), :] = jnp.zeros((length - seen, dk.shape[1]), jnp.float32)
            dv_acc[pl.ds(seen, length - seen), :] = jnp.zeros((length - seen, dv.shape[1]), jnp.float32)
        if start == 0:
            dk_acc[pl.ds(0, seen), :] = dk
            dv_acc[pl.ds(0, seen), :] = dv
        else:
            dk_acc[pl.ds(0, seen), :] += dk
            dv_acc[pl.ds(0, seen), :] += dv
    store(1, 0, (dk_acc[pl.ds(0, length), :] * scale).astype(jnp.bfloat16))
    store(2, 0, dv_acc[pl.ds(0, length), :].astype(jnp.bfloat16))


def kernel(plan, *refs):
    space_in, time_in = refs[0:4], refs[4:8]
    space_out, time_out = refs[8:11], refs[11:14]
    (sp, sp_res, tm, tm_res, dk_acc, dv_acc) = refs[14:20]
    (sp_recv, sp_send, spb_recv, spb_send, tm_recv, tm_send, tmb_recv, tmb_send) = refs[20:]
    n_patch, n_frame, per_dev, rows, frames, heads_dev, span, scale = plan
    length = n_patch * rows
    me_p = lax.axis_index("patch")
    me_f = lax.axis_index("frame")

    def patch_peer(step):
        return lax.rem(me_p + step, n_patch)

    def frame_peer(step):
        return lax.rem(me_f + step, n_frame)

    def time_slot(owner):
        if span == rows:
            return pl.ds(owner * heads_dev, heads_dev), pl.ds(0, span)
        cuts = rows // span
        return (
            pl.ds(owner // cuts, 1),
            pl.ds(pl.multiple_of(lax.rem(owner, cuts) * span, span), span),
        )

    barrier = pltpu.get_barrier_semaphore()
    for step in range(1, n_patch):
        pl.semaphore_signal(barrier, inc=1, device_id={"patch": patch_peer(step)}, device_id_type=MESH)
    for step in range(1, n_frame):
        pl.semaphore_signal(barrier, inc=1, device_id={"frame": frame_peer(step)}, device_id_type=MESH)
    pl.semaphore_wait(barrier, n_patch + n_frame - 2)

    my_rows = pl.ds(pl.multiple_of(me_p * rows, rows), rows)
    pieces = max(1, per_dev // 2)
    piece_frames = frames // pieces

    def send_space(c):
        for step in range(1, n_patch):
            peer = patch_peer(step)
            for a in range(4):
                pltpu.make_async_remote_copy(
                    src_ref=space_in[a].at[peer * per_dev + c],
                    dst_ref=sp.at[c, a, my_rows],
                    send_sem=sp_send.at[c],
                    recv_sem=sp_recv.at[c],
                    device_id={"patch": peer},
                    device_id_type=MESH,
                ).start()
        for a in range(4):
            pltpu.make_async_copy(
                space_in[a].at[me_p * per_dev + c], sp.at[c, a, my_rows], sp_recv.at[c]
            ).start()

    def send_time(c):
        here = pl.ds(c * piece_frames, piece_frames)
        there = pl.ds(me_f * frames + c * piece_frames, piece_frames)
        for step in range(1, n_frame):
            peer = frame_peer(step)
            hs, ps = time_slot(peer)
            for a in range(4):
                pltpu.make_async_remote_copy(
                    src_ref=time_in[a].at[here, hs, ps],
                    dst_ref=tm.at[a, there],
                    send_sem=tm_send.at[0],
                    recv_sem=tm_recv.at[0],
                    device_id={"frame": peer},
                    device_id_type=MESH,
                ).start()
        hs, ps = time_slot(me_f)
        for a in range(4):
            pltpu.make_async_copy(time_in[a].at[here, hs, ps], tm.at[a, there], tm_recv.at[0]).start()

    @pl.loop(0, pieces)
    def _(c):
        send_space(c)
        send_time(c)

    @pl.loop(pieces, per_dev)
    def _(c):
        send_space(c)

    def all_time():
        pltpu.make_async_copy(tm, tm, tm_recv.at[0]).wait()
        units = span // ROWS
        total = n_frame * frames

        @pl.loop(0, heads_dev * units)
        def _(u):
            hh = u // units
            ps = pl.ds(pl.multiple_of(lax.rem(u, units) * ROWS, ROWS), ROWS)

            def load(a, start, count):
                block = tm[a, pl.ds(start // ROWS, count // ROWS), hh, ps, :]
                return block.reshape(count, block.shape[-1])

            def store(a, start, value):
                count = value.shape[0]
                tm_res[a, pl.ds(start // ROWS, count // ROWS), hh, ps, :] = value.reshape(
                    count // ROWS, ROWS, value.shape[1]
                )

            attend(total * ROWS, scale, ROWS, load, store, dk_acc, dv_acc)

        hs, ps = time_slot(me_f)
        for step in range(1, n_frame):
            peer = frame_peer(step)
            for a in range(3):
                pltpu.make_async_remote_copy(
                    src_ref=tm_res.at[a, pl.ds(peer * frames, frames)],
                    dst_ref=time_out[a].at[:, hs, ps],
                    send_sem=tmb_send.at[0],
                    recv_sem=tmb_recv.at[a],
                    device_id={"frame": peer},
                    device_id_type=MESH,
                ).start()
        for a in range(3):
            pltpu.make_async_copy(
                tm_res.at[a, pl.ds(me_f * frames, frames)], time_out[a].at[:, hs, ps], tmb_recv.at[a]
            ).start()

    @pl.loop(0, per_dev)
    def _(c):
        @pl.when(c == pieces)
        def _():
            all_time()

        pltpu.make_async_copy(sp.at[c], sp.at[c], sp_recv.at[c]).wait()

        def load(a, start, count):
            return sp[c, a, pl.ds(start, count), :]

        def store(a, start, value):
            sp_res[c, a, pl.ds(start, value.shape[0]), :] = value

        attend(length, scale, 0, load, store, dk_acc, dv_acc)
        seq = me_p * per_dev + c
        for step in range(1, n_patch):
            peer = patch_peer(step)
            for a in range(3):
                pltpu.make_async_remote_copy(
                    src_ref=sp_res.at[c, a, pl.ds(pl.multiple_of(peer * rows, rows), rows)],
                    dst_ref=space_out[a].at[seq],
                    send_sem=spb_send.at[c],
                    recv_sem=spb_recv.at[a],
                    device_id={"patch": peer},
                    device_id_type=MESH,
                ).start()
        for a in range(3):
            pltpu.make_async_copy(sp_res.at[c, a, my_rows], space_out[a].at[seq], spb_recv.at[a]).start()

    others = pl.ds(0, length - rows)
    away = pl.ds(0, (n_frame - 1) * frames)

    @pl.loop(0, per_dev)
    def _(c):
        pltpu.make_async_copy(sp.at[c, :, others], sp.at[c, :, others], sp_send.at[c]).wait()
        pltpu.make_async_copy(sp_res.at[c, :, others], sp_res.at[c, :, others], spb_send.at[c]).wait()

    pltpu.make_async_copy(tm.at[:, away], tm.at[:, away], tm_send.at[0]).wait()
    pltpu.make_async_copy(tm_res.at[:, away], tm_res.at[:, away], tmb_send.at[0]).wait()
    for a in range(3):
        pltpu.make_async_copy(time_out[a], time_out[a], tmb_recv.at[a]).wait()
        pltpu.make_async_copy(space_out[a], space_out[a], spb_recv.at[a]).wait()


def copy_out(*refs):
    sources, targets, sems = refs[:6], refs[6:12], refs[12]
    copies = [
        pltpu.make_async_copy(source, target, sems.at[i])
        for i, (source, target) in enumerate(zip(sources, targets))
    ]
    for copy in copies:
        copy.start()
    for copy in copies:
        copy.wait()


def per_device(n_frame, n_patch, *blocks):
    frames, heads, rows, dim = blocks[0].shape
    per_dev = frames * heads // n_patch
    if n_frame <= heads:
        heads_dev, span = heads // n_frame, rows
    else:
        heads_dev, span = 1, rows * heads // n_frame
    length = n_patch * rows
    total = n_frame * frames
    scale = 1.0 / math.sqrt(dim)
    plan = (n_patch, n_frame, per_dev, rows, frames, heads_dev, span, scale)
    longest = max(length, total * ROWS)
    flat = (frames * heads, rows, dim)
    whole = (frames, heads, rows, dim)
    bf16 = jnp.bfloat16
    hbm = pl.BlockSpec(memory_space=pltpu.HBM)
    vmem = pl.BlockSpec(memory_space=pltpu.VMEM)
    dma = pltpu.SemaphoreType.DMA
    sent = [b.reshape(flat) for b in blocks[:4]] + list(blocks[4:])
    outs = pl.pallas_call(
        functools.partial(kernel, plan),
        out_shape=[pltpu.VMEM(flat, bf16)] * 3 + [pltpu.VMEM(whole, bf16)] * 3,
        in_specs=[hbm] * 8,
        out_specs=[vmem] * 6,
        scratch_shapes=[
            pltpu.VMEM((per_dev, 4, length, dim), bf16),
            pltpu.VMEM((per_dev, 3, length, dim), bf16),
            pltpu.VMEM((4, total, heads_dev, span, dim), bf16),
            pltpu.VMEM((3, total, heads_dev, span, dim), bf16),
            pltpu.VMEM((longest, dim), jnp.float32),
            pltpu.VMEM((longest, dim), jnp.float32),
            dma((per_dev,)),
            dma((per_dev,)),
            dma((3,)),
            dma((per_dev,)),
            dma((1,)),
            dma((1,)),
            dma((3,)),
            dma((1,)),
        ],
        compiler_params=pltpu.CompilerParams(
            collective_id=0, has_side_effects=True, vmem_limit_bytes=40 * 1024 * 1024
        ),
    )(*[pltpu.with_memory_space_constraint(b, pltpu.HBM) for b in sent])
    return pl.pallas_call(
        copy_out,
        out_shape=[jax.ShapeDtypeStruct(whole, bf16)] * 6,
        in_specs=[vmem] * 6,
        out_specs=[hbm] * 6,
        scratch_shapes=[dma((6,))],
    )(*[o.reshape(whole) for o in outs])


def solution(mesh):
    spec = P("frame", None, "patch", None)
    return jax.shard_map(
        functools.partial(per_device, mesh.shape["frame"], mesh.shape["patch"]),
        mesh=mesh,
        in_specs=(spec,) * 8,
        out_specs=(spec,) * 6,
        check_vma=False,
    )
```

```python
import functools
import math

import jax
import jax.numpy as jnp
from jax import lax
from jax.experimental import pallas as pl
from jax.experimental.pallas import tpu as pltpu
from jax.sharding import PartitionSpec as P

MESH = pl.DeviceIdType.MESH
ROWS = 16
BLOCK = 256


def flip_dot(left, right):
    return lax.dot_general(
        left, right, (((1,), (1,)), ((), ())), preferred_element_type=jnp.float32
    )


def lead_dot(left, right):
    return lax.dot_general(
        left, right, (((0,), (0,)), ((), ())), preferred_element_type=jnp.float32
    )


def attend(length, scale, group, load, store, dk_acc, dv_acc):
    for start in range(0, length, BLOCK):
        rows = min(BLOCK, length - start)
        seen = start + rows if group else length
        query = load(0, start, rows)
        keys = load(1, 0, seen)
        values = load(2, 0, seen)
        upstream = load(3, start, rows)
        scores = flip_dot(keys, query) * scale
        if group:
            gap = (
                lax.broadcasted_iota(jnp.int32, (seen, rows), 1)
                + start
                - lax.broadcasted_iota(jnp.int32, (seen, rows), 0)
            )
            allowed = jnp.logical_and(gap >= 0, (gap & (group - 1)) == 0)
            scores = jnp.where(allowed, scores, -1e30)
        raised = jnp.exp(scores - jnp.max(scores, axis=0, keepdims=True))
        soft = raised * (1.0 / jnp.sum(raised, axis=0, keepdims=True))
        weights = soft.astype(jnp.bfloat16)
        grad_prob = flip_dot(values, upstream)
        delta = jnp.sum(weights.astype(jnp.float32) * grad_prob, axis=0, keepdims=True)
        grad_score = (soft * (grad_prob - delta)).astype(jnp.bfloat16)
        dv = jnp.dot(weights, upstream, preferred_element_type=jnp.float32)
        dk = jnp.dot(grad_score, query, preferred_element_type=jnp.float32)
        store(0, start, (lead_dot(grad_score, keys) * scale).astype(jnp.bfloat16))
        if start == 0 and seen < length:
            dk_acc[pl.ds(seen, length - seen), :] = jnp.zeros((length - seen, dk.shape[1]), jnp.float32)
            dv_acc[pl.ds(seen, length - seen), :] = jnp.zeros((length - seen, dv.shape[1]), jnp.float32)
        if start == 0:
            dk_acc[pl.ds(0, seen), :] = dk
            dv_acc[pl.ds(0, seen), :] = dv
        else:
            dk_acc[pl.ds(0, seen), :] += dk
            dv_acc[pl.ds(0, seen), :] += dv
    store(1, 0, (dk_acc[pl.ds(0, length), :] * scale).astype(jnp.bfloat16))
    store(2, 0, dv_acc[pl.ds(0, length), :].astype(jnp.bfloat16))


def half_scores(part_keys, part_values, query, upstream, scale):
    scores = flip_dot(part_keys, query) * scale
    top = jnp.max(scores, axis=0, keepdims=True)
    raised = jnp.exp(scores - top)
    grad_prob = flip_dot(part_values, upstream)
    mass = jnp.sum(raised, axis=0, keepdims=True)
    drift = jnp.sum(raised * grad_prob, axis=0, keepdims=True)
    return raised, grad_prob, top, mass, drift


def kernel(plan, *refs):
    space_in, time_in = refs[0:4], refs[4:8]
    space_out, time_out = refs[8:11], refs[11:14]
    sp, xp, res, dq_out, dq_in, dq_own, st_out, st_in, e_ring, p_ring = refs[14:24]
    tm, tm_res, dk_acc, dv_acc = refs[24:28]
    (sp_recv, sp_send, xp_recv, xp_send, st_recv, st_send, dq_recv, dq_send) = refs[28:36]
    (res_recv, res_send, tm_recv, tm_send, tmb_recv, tmb_send) = refs[36:]
    n_patch, n_frame, n_seq, rows, frames, heads_dev, span, lag, scale = plan
    half_devs, n_proc = n_patch // 2, n_patch // 4
    per_proc = n_seq // n_proc
    half_rows = half_devs * rows
    ring = lag + 1
    me_p = lax.axis_index("patch")
    me_f = lax.axis_index("frame")
    half = me_p // half_devs
    slot = me_p - half * half_devs
    first_proc = half_devs - n_proc + half * n_proc
    partner = me_p + n_proc - 2 * n_proc * half
    is_proc = jnp.logical_and(me_p >= half_devs - n_proc, me_p < half_devs + n_proc)

    def frame_peer(step):
        return lax.rem(me_f + step, n_frame)

    def time_slot(owner):
        if span == rows:
            return pl.ds(owner * heads_dev, heads_dev), pl.ds(0, span)
        cuts = rows // span
        return (
            pl.ds(owner // cuts, 1),
            pl.ds(pl.multiple_of(lax.rem(owner, cuts) * span, span), span),
        )

    def send(src, dst, send_sem, recv_sem, where):
        pltpu.make_async_remote_copy(
            src_ref=src,
            dst_ref=dst,
            send_sem=send_sem,
            recv_sem=recv_sem,
            device_id=where,
            device_id_type=MESH,
        ).start()

    def wait_bytes(ref, sem):
        pltpu.make_async_copy(ref, ref, sem).wait()

    barrier = pltpu.get_barrier_semaphore()
    for step in range(1, n_patch):
        peer = lax.rem(me_p + step, n_patch)
        pl.semaphore_signal(barrier, inc=1, device_id={"patch": peer}, device_id_type=MESH)
    for step in range(1, n_frame):
        pl.semaphore_signal(barrier, inc=1, device_id={"frame": frame_peer(step)}, device_id_type=MESH)
    pl.semaphore_wait(barrier, n_patch + n_frame - 2)

    my_rows = pl.ds(pl.multiple_of(slot * rows, rows), rows)
    place = (0, 2, 3, 1)

    def send_space(c):
        for j in range(n_proc):
            proc = first_proc + j
            for a in range(4):
                source = space_in[a].at[j * per_proc + c]
                target = sp.at[c, place[a], my_rows]

                @pl.when(proc != me_p)
                def _():
                    send(source, target, sp_send.at[a], sp_recv.at[c], {"patch": proc})

                @pl.when(proc == me_p)
                def _():
                    pltpu.make_async_copy(source, target, sp_recv.at[c]).start()

    def send_time(c):
        here = pl.ds(c, 1)
        there = pl.ds(me_f * frames + c, 1)
        for step in range(1, n_frame):
            peer = frame_peer(step)
            hs, ps = time_slot(peer)
            for a in range(4):
                send(
                    time_in[a].at[here, hs, ps], tm.at[a, there], tm_send.at[0], tm_recv.at[0], {"frame": peer}
                )
        hs, ps = time_slot(me_f)
        for a in range(4):
            pltpu.make_async_copy(time_in[a].at[here, hs, ps], tm.at[a, there], tm_recv.at[0]).start()

    @pl.loop(0, frames)
    def _(c):
        send_space(c)
        send_time(c)

    @pl.loop(frames, per_proc)
    def _(c):
        send_space(c)

    units = span // ROWS
    total = n_frame * frames
    time_units = heads_dev * units

    def time_unit(u):
        hh = u // units
        ps = pl.ds(pl.multiple_of(lax.rem(u, units) * ROWS, ROWS), ROWS)

        def load(a, start, count):
            block = tm[a, pl.ds(start // ROWS, count // ROWS), hh, ps, :]
            return block.reshape(count, block.shape[-1])

        def store(a, start, value):
            count = value.shape[0]
            tm_res[a, pl.ds(start // ROWS, count // ROWS), hh, ps, :] = value.reshape(
                count // ROWS, ROWS, value.shape[1]
            )

        attend(total * ROWS, scale, ROWS, load, store, dk_acc, dv_acc)

    def return_time():
        hs, ps = time_slot(me_f)
        for step in range(1, n_frame):
            peer = frame_peer(step)
            for a in range(3):
                send(
                    tm_res.at[a, pl.ds(peer * frames, frames)],
                    time_out[a].at[:, hs, ps],
                    tmb_send.at[0],
                    tmb_recv.at[a],
                    {"frame": peer},
                )
        for a in range(3):
            pltpu.make_async_copy(
                tm_res.at[a, pl.ds(me_f * frames, frames)], time_out[a].at[:, hs, ps], tmb_recv.at[a]
            ).start()

    def relay(k):
        wait_bytes(sp.at[k], sp_recv.at[k])
        send(sp.at[k, pl.ds(0, 2)], xp.at[k], xp_send.at[0], xp_recv.at[k], {"patch": partner})

    def sides(k):
        return ((sp[k, 0], sp[k, 1]), (xp[k, 0], xp[k, 1]))

    def first_pass(k):
        wait_bytes(xp.at[k], xp_recv.at[k])
        at = lax.rem(k, ring)
        for side, (query, upstream) in enumerate(sides(k)):
            raised, grad_prob, top, mass, drift = half_scores(sp[k, 2], sp[k, 3], query, upstream, scale)
            e_ring[at, side] = raised
            p_ring[at, side] = grad_prob
            st_out[k, side] = jnp.broadcast_to(top, (8, half_rows))
            st_out[k, side, pl.ds(1, 1), :] = mass
            st_out[k, side, pl.ds(2, 1), :] = drift
        send(st_out.at[k], st_in.at[k], st_send.at[0], st_recv.at[k], {"patch": partner})

    def give(k, a):
        seq = (me_p - first_proc) * per_proc + k
        for step in range(1, half_devs):
            other = lax.rem(slot + step, half_devs)
            send(
                res.at[k, a, pl.ds(pl.multiple_of(other * rows, rows), rows)],
                space_out[a].at[seq],
                res_send.at[a],
                res_recv.at[a],
                {"patch": half * half_devs + other},
            )
        pltpu.make_async_copy(res.at[k, a, my_rows], space_out[a].at[seq], res_recv.at[a]).start()

    def second_pass(k):
        wait_bytes(st_in.at[k], st_recv.at[k])
        at = lax.rem(k, ring)
        keys = sp[k, 2]
        dk = dv = None
        for side, (query, upstream) in enumerate(sides(k)):
            mine, theirs = st_out[k, side], st_in[k, 1 - side]
            top = jnp.maximum(mine[0:1], theirs[0:1])
            my_part, their_part = jnp.exp(mine[0:1] - top), jnp.exp(theirs[0:1] - top)
            inverse = 1.0 / (mine[1:2] * my_part + theirs[1:2] * their_part)
            delta = (mine[2:3] * my_part + theirs[2:3] * their_part) * inverse
            soft = e_ring[at, side] * (my_part * inverse)
            weights = soft.astype(jnp.bfloat16)
            grad_score = (soft * (p_ring[at, side] - delta)).astype(jnp.bfloat16)
            dv_side = jnp.dot(weights, upstream, preferred_element_type=jnp.float32)
            dk_side = jnp.dot(grad_score, query, preferred_element_type=jnp.float32)
            dk = dk_side if dk is None else dk + dk_side
            dv = dv_side if dv is None else dv + dv_side
            dq = lead_dot(grad_score, keys) * scale
            if side == 0:
                dq_own[at] = dq
            else:
                dq_out[k] = dq.astype(jnp.bfloat16)
        send(dq_out.at[k], dq_in.at[k], dq_send.at[0], dq_recv.at[k], {"patch": partner})
        res[k, 1] = (dk * scale).astype(jnp.bfloat16)
        res[k, 2] = dv.astype(jnp.bfloat16)
        give(k, 1)
        give(k, 2)

    def finish(k):
        wait_bytes(dq_in.at[k], dq_recv.at[k])
        res[k, 0] = (dq_own[lax.rem(k, ring)] + dq_in[k].astype(jnp.float32)).astype(jnp.bfloat16)
        give(k, 0)

    time_start = per_proc // 2

    @pl.loop(0, per_proc + 3 * lag)
    def _(t):
        for stage, work in enumerate((relay, first_pass, second_pass, finish)):
            k = t - stage * lag

            @pl.when(jnp.logical_and(is_proc, jnp.logical_and(k >= 0, k < per_proc)))
            def _():
                work(k)

        @pl.when(t == time_start)
        def _():
            wait_bytes(tm, tm_recv.at[0])

        @pl.when(jnp.logical_and(t >= time_start, t < time_start + time_units))
        def _():
            time_unit(t - time_start)

        @pl.when(t == time_start + time_units)
        def _():
            return_time()

    @pl.when(is_proc)
    def _():
        for a in range(4):
            if n_seq > per_proc:
                wait_bytes(space_in[a].at[pl.ds(0, n_seq - per_proc)], sp_send.at[a])
        wait_bytes(xp, xp_send.at[0])
        wait_bytes(st_in, st_send.at[0])
        wait_bytes(dq_in, dq_send.at[0])
        for a in range(3):
            wait_bytes(res.at[:, a, pl.ds(0, half_rows - rows)], res_send.at[a])

    @pl.when(jnp.logical_not(is_proc))
    def _():
        for a in range(4):
            wait_bytes(space_in[a], sp_send.at[a])

    away = pl.ds(0, (n_frame - 1) * frames)
    wait_bytes(tm.at[:, away], tm_send.at[0])
    wait_bytes(tm_res.at[:, away], tmb_send.at[0])
    for a in range(3):
        wait_bytes(time_out[a], tmb_recv.at[a])
        wait_bytes(space_out[a], res_recv.at[a])


def copy_out(*refs):
    sources, targets, sems = refs[:6], refs[6:12], refs[12]
    copies = [
        pltpu.make_async_copy(source, target, sems.at[i])
        for i, (source, target) in enumerate(zip(sources, targets))
    ]
    for copy in copies:
        copy.start()
    for copy in copies:
        copy.wait()


def per_device(n_frame, n_patch, *blocks):
    frames, heads, rows, dim = blocks[0].shape
    n_seq = frames * heads
    per_proc = n_seq // (n_patch // 4)
    half_rows = n_patch // 2 * rows
    lag = 3 if half_rows <= 256 else 1
    if n_frame <= heads:
        heads_dev, span = heads // n_frame, rows
    else:
        heads_dev, span = 1, rows * heads // n_frame
    total = n_frame * frames
    scale = 1.0 / math.sqrt(dim)
    plan = (n_patch, n_frame, n_seq, rows, frames, heads_dev, span, lag, scale)
    longest = total * ROWS
    f32 = jnp.float32
    flat = (frames * heads, rows, dim)
    whole = (frames, heads, rows, dim)
    bf16 = jnp.bfloat16
    hbm = pl.BlockSpec(memory_space=pltpu.HBM)
    vmem = pl.BlockSpec(memory_space=pltpu.VMEM)
    dma = pltpu.SemaphoreType.DMA
    sent = [b.reshape(flat) for b in blocks[:4]] + list(blocks[4:])
    outs = pl.pallas_call(
        functools.partial(kernel, plan),
        out_shape=[pltpu.VMEM(flat, bf16)] * 3 + [pltpu.VMEM(whole, bf16)] * 3,
        in_specs=[hbm] * 8,
        out_specs=[vmem] * 6,
        scratch_shapes=[
            pltpu.VMEM((per_proc, 4, half_rows, dim), bf16),
            pltpu.VMEM((per_proc, 2, half_rows, dim), bf16),
            pltpu.VMEM((per_proc, 3, half_rows, dim), bf16),
            pltpu.VMEM((per_proc, half_rows, dim), bf16),
            pltpu.VMEM((per_proc, half_rows, dim), bf16),
            pltpu.VMEM((lag + 1, half_rows, dim), f32),
            pltpu.VMEM((per_proc, 2, 8, half_rows), f32),
            pltpu.VMEM((per_proc, 2, 8, half_rows), f32),
            pltpu.VMEM((lag + 1, 2, half_rows, half_rows), f32),
            pltpu.VMEM((lag + 1, 2, half_rows, half_rows), f32),
            pltpu.VMEM((4, total, heads_dev, span, dim), bf16),
            pltpu.VMEM((3, total, heads_dev, span, dim), bf16),
            pltpu.VMEM((longest, dim), f32),
            pltpu.VMEM((longest, dim), f32),
            dma((per_proc,)),
            dma((4,)),
            dma((per_proc,)),
            dma((1,)),
            dma((per_proc,)),
            dma((1,)),
            dma((per_proc,)),
            dma((1,)),
            dma((3,)),
            dma((3,)),
            dma((1,)),
            dma((1,)),
            dma((3,)),
            dma((1,)),
        ],
        compiler_params=pltpu.CompilerParams(
            collective_id=0, has_side_effects=True, vmem_limit_bytes=52 * 1024 * 1024
        ),
    )(*[pltpu.with_memory_space_constraint(b, pltpu.HBM) for b in sent])
    return pl.pallas_call(
        copy_out,
        out_shape=[jax.ShapeDtypeStruct(whole, bf16)] * 6,
        in_specs=[vmem] * 6,
        out_specs=[hbm] * 6,
        scratch_shapes=[dma((6,))],
        compiler_params=pltpu.CompilerParams(vmem_limit_bytes=1024 * 1024),
    )(*[o.reshape(whole) for o in outs])


def solution(mesh):
    spec = P("frame", None, "patch", None)
    return jax.shard_map(
        functools.partial(per_device, mesh.shape["frame"], mesh.shape["patch"]),
        mesh=mesh,
        in_specs=(spec,) * 8,
        out_specs=(spec,) * 6,
        check_vma=False,
    )
```

```python
import functools
import math

import jax
import jax.numpy as jnp
from jax import lax
from jax.experimental import pallas as pl
from jax.experimental.pallas import tpu as pltpu
from jax.sharding import PartitionSpec as P

MESH = pl.DeviceIdType.MESH
ROWS = 16
BLOCK = 256


def flip_dot(left, right):
    return lax.dot_general(
        left, right, (((1,), (1,)), ((), ())), preferred_element_type=jnp.float32
    )


def lead_dot(left, right):
    return lax.dot_general(
        left, right, (((0,), (0,)), ((), ())), preferred_element_type=jnp.float32
    )


def attend(length, scale, group, load, store, dk_acc, dv_acc):
    for start in range(0, length, BLOCK):
        rows = min(BLOCK, length - start)
        seen = start + rows if group else length
        query = load(0, start, rows)
        keys = load(1, 0, seen)
        values = load(2, 0, seen)
        upstream = load(3, start, rows)
        scores = flip_dot(keys, query) * scale
        if group:
            gap = (
                lax.broadcasted_iota(jnp.int32, (seen, rows), 1)
                + start
                - lax.broadcasted_iota(jnp.int32, (seen, rows), 0)
            )
            allowed = jnp.logical_and(gap >= 0, (gap & (group - 1)) == 0)
            scores = jnp.where(allowed, scores, -1e30)
        raised = jnp.exp(scores - jnp.max(scores, axis=0, keepdims=True))
        soft = raised * (1.0 / jnp.sum(raised, axis=0, keepdims=True))
        weights = soft.astype(jnp.bfloat16)
        grad_prob = flip_dot(values, upstream)
        delta = jnp.sum(weights.astype(jnp.float32) * grad_prob, axis=0, keepdims=True)
        grad_score = (soft * (grad_prob - delta)).astype(jnp.bfloat16)
        dv = jnp.dot(weights, upstream, preferred_element_type=jnp.float32)
        dk = jnp.dot(grad_score, query, preferred_element_type=jnp.float32)
        store(0, start, (lead_dot(grad_score, keys) * scale).astype(jnp.bfloat16))
        if start == 0 and seen < length:
            dk_acc[pl.ds(seen, length - seen), :] = jnp.zeros((length - seen, dk.shape[1]), jnp.float32)
            dv_acc[pl.ds(seen, length - seen), :] = jnp.zeros((length - seen, dv.shape[1]), jnp.float32)
        if start == 0:
            dk_acc[pl.ds(0, seen), :] = dk
            dv_acc[pl.ds(0, seen), :] = dv
        else:
            dk_acc[pl.ds(0, seen), :] += dk
            dv_acc[pl.ds(0, seen), :] += dv
    store(1, 0, (dk_acc[pl.ds(0, length), :] * scale).astype(jnp.bfloat16))
    store(2, 0, dv_acc[pl.ds(0, length), :].astype(jnp.bfloat16))


def half_scores(part_keys, part_values, query, upstream, scale):
    scores = flip_dot(part_keys, query) * scale
    top = jnp.max(scores, axis=0, keepdims=True)
    raised = jnp.exp(scores - top)
    grad_prob = flip_dot(part_values, upstream)
    mass = jnp.sum(raised, axis=0, keepdims=True)
    drift = jnp.sum(raised * grad_prob, axis=0, keepdims=True)
    return raised, grad_prob, top, mass, drift


def kernel(plan, *refs):
    space_in, time_in = refs[0:4], refs[4:8]
    space_out, time_out = refs[8:11], refs[11:14]
    sp, xp, res, dq_out, dq_in, dq_own, st_out, st_in, e_ring, p_ring = refs[14:24]
    tm, tm_res, dk_acc, dv_acc = refs[24:28]
    (sp_recv, sp_send, xp_recv, xp_send, st_recv, st_send, dq_recv, dq_send) = refs[28:36]
    (res_recv, res_send, tm_recv, tm_send, tmb_recv, tmb_send) = refs[36:]
    n_patch, n_frame, n_seq, rows, frames, heads_dev, span, lag, scale = plan
    half_devs, n_proc = n_patch // 2, n_patch // 4
    per_proc = n_seq // n_proc
    half_rows = half_devs * rows
    ring = lag + 1
    me_p = lax.axis_index("patch")
    me_f = lax.axis_index("frame")
    half = me_p // half_devs
    slot = me_p - half * half_devs
    first_proc = half_devs - n_proc + half * n_proc
    partner = me_p + n_proc - 2 * n_proc * half
    is_proc = jnp.logical_and(me_p >= half_devs - n_proc, me_p < half_devs + n_proc)

    def frame_peer(step):
        return lax.rem(me_f + step, n_frame)

    def time_slot(owner):
        if span == rows:
            return pl.ds(owner * heads_dev, heads_dev), pl.ds(0, span)
        cuts = rows // span
        return (
            pl.ds(owner // cuts, 1),
            pl.ds(pl.multiple_of(lax.rem(owner, cuts) * span, span), span),
        )

    def send(src, dst, send_sem, recv_sem, where):
        pltpu.make_async_remote_copy(
            src_ref=src,
            dst_ref=dst,
            send_sem=send_sem,
            recv_sem=recv_sem,
            device_id=where,
            device_id_type=MESH,
        ).start()

    def wait_bytes(ref, sem):
        pltpu.make_async_copy(ref, ref, sem).wait()

    barrier = pltpu.get_barrier_semaphore()
    for step in range(1, n_patch):
        peer = lax.rem(me_p + step, n_patch)
        pl.semaphore_signal(barrier, inc=1, device_id={"patch": peer}, device_id_type=MESH)
    for step in range(1, n_frame):
        pl.semaphore_signal(barrier, inc=1, device_id={"frame": frame_peer(step)}, device_id_type=MESH)
    pl.semaphore_wait(barrier, n_patch + n_frame - 2)

    my_rows = pl.ds(pl.multiple_of(slot * rows, rows), rows)
    place = (0, 2, 3, 1)

    def send_space(c):
        for j in range(n_proc):
            proc = first_proc + j
            for a in range(4):
                source = space_in[a].at[j * per_proc + c]
                target = sp.at[c, place[a], my_rows]

                @pl.when(proc != me_p)
                def _():
                    send(source, target, sp_send.at[a], sp_recv.at[c], {"patch": proc})

                @pl.when(proc == me_p)
                def _():
                    pltpu.make_async_copy(source, target, sp_recv.at[c]).start()

    def send_time(c):
        here = pl.ds(c, 1)
        there = pl.ds(me_f * frames + c, 1)
        for step in range(1, n_frame):
            peer = frame_peer(step)
            hs, ps = time_slot(peer)
            for a in range(4):
                send(
                    time_in[a].at[here, hs, ps], tm.at[a, there], tm_send.at[0], tm_recv.at[0], {"frame": peer}
                )
        hs, ps = time_slot(me_f)
        for a in range(4):
            pltpu.make_async_copy(time_in[a].at[here, hs, ps], tm.at[a, there], tm_recv.at[0]).start()

    ahead = min(6, per_proc)
    stride = max(1, per_proc // (2 * frames))

    def paced_time(c):
        @pl.when(jnp.logical_and(lax.rem(c, stride) == 0, c < frames * stride))
        def _():
            send_time(c // stride)

    @pl.when(is_proc)
    def _():
        @pl.loop(0, ahead)
        def _(c):
            send_space(c)

    @pl.when(jnp.logical_not(is_proc))
    def _():
        @pl.loop(0, per_proc)
        def _(c):
            send_space(c)
            paced_time(c)

    units = span // ROWS
    total = n_frame * frames
    time_units = heads_dev * units

    def time_unit(u):
        hh = u // units
        ps = pl.ds(pl.multiple_of(lax.rem(u, units) * ROWS, ROWS), ROWS)

        def load(a, start, count):
            block = tm[a, pl.ds(start // ROWS, count // ROWS), hh, ps, :]
            return block.reshape(count, block.shape[-1])

        def store(a, start, value):
            count = value.shape[0]
            tm_res[a, pl.ds(start // ROWS, count // ROWS), hh, ps, :] = value.reshape(
                count // ROWS, ROWS, value.shape[1]
            )

        attend(total * ROWS, scale, ROWS, load, store, dk_acc, dv_acc)

    def return_time(hh):
        if span == rows:
            hs, ps = pl.ds(me_f * heads_dev + hh, 1), pl.ds(0, span)
        else:
            hs, ps = time_slot(me_f)
        head = pl.ds(hh, 1)
        for step in range(1, n_frame):
            peer = frame_peer(step)
            for a in range(3):
                send(
                    tm_res.at[a, pl.ds(peer * frames, frames), head],
                    time_out[a].at[:, hs, ps],
                    tmb_send.at[0],
                    tmb_recv.at[a],
                    {"frame": peer},
                )
        for a in range(3):
            pltpu.make_async_copy(
                tm_res.at[a, pl.ds(me_f * frames, frames), head], time_out[a].at[:, hs, ps], tmb_recv.at[a]
            ).start()

    def relay(k):
        wait_bytes(sp.at[k], sp_recv.at[k])
        send(sp.at[k, pl.ds(0, 2)], xp.at[k], xp_send.at[0], xp_recv.at[k], {"patch": partner})

    def sides(k):
        return ((sp[k, 0], sp[k, 1]), (xp[k, 0], xp[k, 1]))

    def first_pass(k):
        wait_bytes(xp.at[k], xp_recv.at[k])
        at = lax.rem(k, ring)
        for side, (query, upstream) in enumerate(sides(k)):
            raised, grad_prob, top, mass, drift = half_scores(sp[k, 2], sp[k, 3], query, upstream, scale)
            e_ring[at, side] = raised
            p_ring[at, side] = grad_prob
            st_out[k, side] = jnp.broadcast_to(top, (8, half_rows))
            st_out[k, side, pl.ds(1, 1), :] = mass
            st_out[k, side, pl.ds(2, 1), :] = drift
        send(st_out.at[k], st_in.at[k], st_send.at[0], st_recv.at[k], {"patch": partner})

    def give(k, a):
        seq = (me_p - first_proc) * per_proc + k
        for step in range(1, half_devs):
            other = lax.rem(slot + step, half_devs)
            send(
                res.at[k, a, pl.ds(pl.multiple_of(other * rows, rows), rows)],
                space_out[a].at[seq],
                res_send.at[a],
                res_recv.at[a],
                {"patch": half * half_devs + other},
            )
        pltpu.make_async_copy(res.at[k, a, my_rows], space_out[a].at[seq], res_recv.at[a]).start()

    def second_pass(k):
        wait_bytes(st_in.at[k], st_recv.at[k])
        at = lax.rem(k, ring)
        keys = sp[k, 2]
        dk = dv = None
        for side, (query, upstream) in enumerate(sides(k)):
            mine, theirs = st_out[k, side], st_in[k, 1 - side]
            top = jnp.maximum(mine[0:1], theirs[0:1])
            my_part, their_part = jnp.exp(mine[0:1] - top), jnp.exp(theirs[0:1] - top)
            inverse = 1.0 / (mine[1:2] * my_part + theirs[1:2] * their_part)
            delta = (mine[2:3] * my_part + theirs[2:3] * their_part) * inverse
            soft = e_ring[at, side] * (my_part * inverse)
            weights = soft.astype(jnp.bfloat16)
            grad_score = (soft * (p_ring[at, side] - delta)).astype(jnp.bfloat16)
            dv_side = jnp.dot(weights, upstream, preferred_element_type=jnp.float32)
            dk_side = jnp.dot(grad_score, query, preferred_element_type=jnp.float32)
            dk = dk_side if dk is None else dk + dk_side
            dv = dv_side if dv is None else dv + dv_side
            dq = lead_dot(grad_score, keys) * scale
            if side == 0:
                dq_own[at] = dq
            else:
                dq_out[k] = dq.astype(jnp.bfloat16)
        send(dq_out.at[k], dq_in.at[k], dq_send.at[0], dq_recv.at[k], {"patch": partner})
        res[k, 1] = (dk * scale).astype(jnp.bfloat16)
        res[k, 2] = dv.astype(jnp.bfloat16)
        give(k, 1)
        give(k, 2)

    def finish(k):
        wait_bytes(dq_in.at[k], dq_recv.at[k])
        res[k, 0] = (dq_own[lax.rem(k, ring)] + dq_in[k].astype(jnp.float32)).astype(jnp.bfloat16)
        give(k, 0)

    time_start = per_proc // 2 + 2

    @pl.loop(0, per_proc + 3 * lag)
    def _(t):
        for stage, work in enumerate((relay, first_pass, second_pass, finish)):
            k = t - stage * lag

            @pl.when(jnp.logical_and(is_proc, jnp.logical_and(k >= 0, k < per_proc)))
            def _():
                work(k)

            if stage == 0:

                @pl.when(jnp.logical_and(is_proc, t < per_proc - ahead))
                def _():
                    send_space(t + ahead)

                @pl.when(is_proc)
                def _():
                    paced_time(t)

        @pl.when(t == time_start)
        def _():
            wait_bytes(tm, tm_recv.at[0])

        @pl.when(jnp.logical_and(t >= time_start, t < time_start + time_units))
        def _():
            u = t - time_start
            time_unit(u)

            @pl.when(lax.rem(u, units) == units - 1)
            def _():
                return_time(u // units)

    @pl.when(is_proc)
    def _():
        for a in range(4):
            if n_seq > per_proc:
                wait_bytes(space_in[a].at[pl.ds(0, n_seq - per_proc)], sp_send.at[a])
        wait_bytes(xp, xp_send.at[0])
        wait_bytes(st_in, st_send.at[0])
        wait_bytes(dq_in, dq_send.at[0])
        for a in range(3):
            wait_bytes(res.at[:, a, pl.ds(0, half_rows - rows)], res_send.at[a])

    @pl.when(jnp.logical_not(is_proc))
    def _():
        for a in range(4):
            wait_bytes(space_in[a], sp_send.at[a])

    away = pl.ds(0, (n_frame - 1) * frames)
    wait_bytes(tm.at[:, away], tm_send.at[0])
    wait_bytes(tm_res.at[:, away], tmb_send.at[0])
    for a in range(3):
        wait_bytes(time_out[a], tmb_recv.at[a])
        wait_bytes(space_out[a], res_recv.at[a])


def copy_out(*refs):
    sources, targets, sems = refs[:6], refs[6:12], refs[12]
    copies = [
        pltpu.make_async_copy(source, target, sems.at[i])
        for i, (source, target) in enumerate(zip(sources, targets))
    ]
    for copy in copies:
        copy.start()
    for copy in copies:
        copy.wait()


def per_device(n_frame, n_patch, *blocks):
    frames, heads, rows, dim = blocks[0].shape
    n_seq = frames * heads
    per_proc = n_seq // (n_patch // 4)
    half_rows = n_patch // 2 * rows
    lag = 3 if half_rows <= 256 else 1
    if n_frame <= heads:
        heads_dev, span = heads // n_frame, rows
    else:
        heads_dev, span = 1, rows * heads // n_frame
    total = n_frame * frames
    scale = 1.0 / math.sqrt(dim)
    plan = (n_patch, n_frame, n_seq, rows, frames, heads_dev, span, lag, scale)
    longest = total * ROWS
    f32 = jnp.float32
    flat = (frames * heads, rows, dim)
    whole = (frames, heads, rows, dim)
    bf16 = jnp.bfloat16
    hbm = pl.BlockSpec(memory_space=pltpu.HBM)
    vmem = pl.BlockSpec(memory_space=pltpu.VMEM)
    dma = pltpu.SemaphoreType.DMA
    sent = [b.reshape(flat) for b in blocks[:4]] + list(blocks[4:])
    outs = pl.pallas_call(
        functools.partial(kernel, plan),
        out_shape=[pltpu.VMEM(flat, bf16)] * 3 + [pltpu.VMEM(whole, bf16)] * 3,
        in_specs=[hbm] * 8,
        out_specs=[vmem] * 6,
        scratch_shapes=[
            pltpu.VMEM((per_proc, 4, half_rows, dim), bf16),
            pltpu.VMEM((per_proc, 2, half_rows, dim), bf16),
            pltpu.VMEM((per_proc, 3, half_rows, dim), bf16),
            pltpu.VMEM((per_proc, half_rows, dim), bf16),
            pltpu.VMEM((per_proc, half_rows, dim), bf16),
            pltpu.VMEM((lag + 1, half_rows, dim), f32),
            pltpu.VMEM((per_proc, 2, 8, half_rows), f32),
            pltpu.VMEM((per_proc, 2, 8, half_rows), f32),
            pltpu.VMEM((lag + 1, 2, half_rows, half_rows), f32),
            pltpu.VMEM((lag + 1, 2, half_rows, half_rows), f32),
            pltpu.VMEM((4, total, heads_dev, span, dim), bf16),
            pltpu.VMEM((3, total, heads_dev, span, dim), bf16),
            pltpu.VMEM((longest, dim), f32),
            pltpu.VMEM((longest, dim), f32),
            dma((per_proc,)),
            dma((4,)),
            dma((per_proc,)),
            dma((1,)),
            dma((per_proc,)),
            dma((1,)),
            dma((per_proc,)),
            dma((1,)),
            dma((3,)),
            dma((3,)),
            dma((1,)),
            dma((1,)),
            dma((3,)),
            dma((1,)),
        ],
        compiler_params=pltpu.CompilerParams(
            collective_id=0, has_side_effects=True, vmem_limit_bytes=52 * 1024 * 1024
        ),
    )(*[pltpu.with_memory_space_constraint(b, pltpu.HBM) for b in sent])
    return pl.pallas_call(
        copy_out,
        out_shape=[jax.ShapeDtypeStruct(whole, bf16)] * 6,
        in_specs=[vmem] * 6,
        out_specs=[hbm] * 6,
        scratch_shapes=[dma((6,))],
        compiler_params=pltpu.CompilerParams(vmem_limit_bytes=1024 * 1024),
    )(*[o.reshape(whole) for o in outs])


def solution(mesh):
    spec = P("frame", None, "patch", None)
    return jax.shard_map(
        functools.partial(per_device, mesh.shape["frame"], mesh.shape["patch"]),
        mesh=mesh,
        in_specs=(spec,) * 8,
        out_specs=(spec,) * 6,
        check_vma=False,
    )
```

```python
import functools
import math

import jax
import jax.numpy as jnp
from jax import lax
from jax.experimental import pallas as pl
from jax.experimental.pallas import tpu as pltpu
from jax.sharding import PartitionSpec as P

MESH = pl.DeviceIdType.MESH
ROWS = 16
BLOCK = 256


def flip_dot(left, right):
    return lax.dot_general(
        left, right, (((1,), (1,)), ((), ())), preferred_element_type=jnp.float32
    )


def lead_dot(left, right):
    return lax.dot_general(
        left, right, (((0,), (0,)), ((), ())), preferred_element_type=jnp.float32
    )


def attend(length, scale, group, load, store, dk_acc, dv_acc):
    for start in range(0, length, BLOCK):
        rows = min(BLOCK, length - start)
        seen = start + rows if group else length
        query = load(0, start, rows)
        keys = load(1, 0, seen)
        values = load(2, 0, seen)
        upstream = load(3, start, rows)
        scores = flip_dot(keys, query) * scale
        if group:
            gap = (
                lax.broadcasted_iota(jnp.int32, (seen, rows), 1)
                + start
                - lax.broadcasted_iota(jnp.int32, (seen, rows), 0)
            )
            allowed = jnp.logical_and(gap >= 0, (gap & (group - 1)) == 0)
            scores = jnp.where(allowed, scores, -1e30)
        raised = jnp.exp(scores - jnp.max(scores, axis=0, keepdims=True))
        soft = raised * (1.0 / jnp.sum(raised, axis=0, keepdims=True))
        weights = soft.astype(jnp.bfloat16)
        grad_prob = flip_dot(values, upstream)
        delta = jnp.sum(weights.astype(jnp.float32) * grad_prob, axis=0, keepdims=True)
        grad_score = (soft * (grad_prob - delta)).astype(jnp.bfloat16)
        dv = jnp.dot(weights, upstream, preferred_element_type=jnp.float32)
        dk = jnp.dot(grad_score, query, preferred_element_type=jnp.float32)
        store(0, start, (lead_dot(grad_score, keys) * scale).astype(jnp.bfloat16))
        if start == 0 and seen < length:
            dk_acc[pl.ds(seen, length - seen), :] = jnp.zeros((length - seen, dk.shape[1]), jnp.float32)
            dv_acc[pl.ds(seen, length - seen), :] = jnp.zeros((length - seen, dv.shape[1]), jnp.float32)
        if start == 0:
            dk_acc[pl.ds(0, seen), :] = dk
            dv_acc[pl.ds(0, seen), :] = dv
        else:
            dk_acc[pl.ds(0, seen), :] += dk
            dv_acc[pl.ds(0, seen), :] += dv
    store(1, 0, (dk_acc[pl.ds(0, length), :] * scale).astype(jnp.bfloat16))
    store(2, 0, dv_acc[pl.ds(0, length), :].astype(jnp.bfloat16))


def half_scores(part_keys, part_values, query, upstream, scale):
    scores = flip_dot(part_keys, query) * scale
    top = jnp.max(scores, axis=0, keepdims=True)
    raised = jnp.exp(scores - top)
    grad_prob = flip_dot(part_values, upstream)
    mass = jnp.sum(raised, axis=0, keepdims=True)
    drift = jnp.sum(raised * grad_prob, axis=0, keepdims=True)
    return raised, grad_prob, top, mass, drift


def kernel(plan, *refs):
    space_in, time_in = refs[0:4], refs[4:8]
    space_out, time_out = refs[8:11], refs[11:14]
    sp, xp, res, dq_out, dq_in, dq_own, st_out, st_in, e_ring, p_ring = refs[14:24]
    tm, tm_res, dk_acc, dv_acc = refs[24:28]
    (sp_recv, sp_send, xp_recv, xp_send, st_recv, st_send, dq_recv, dq_send) = refs[28:36]
    (res_recv, res_send, tm_recv, tm_send, tmb_recv, tmb_send) = refs[36:]
    n_patch, n_frame, n_seq, rows, frames, heads_dev, span, lag, scale = plan
    half_devs, n_proc = n_patch // 2, n_patch // 4
    n_out = n_seq // n_proc // 4
    n_mid = n_seq // n_proc - n_out
    ratio = n_mid // n_out
    half_rows = half_devs * rows
    ring = lag + 1
    me_p = lax.axis_index("patch")
    me_f = lax.axis_index("frame")
    half = me_p // half_devs
    slot = me_p - half * half_devs
    mid_slot, out_slot = n_proc * (1 - half), n_proc * half
    is_mid = slot // n_proc == 1 - half
    lane = lax.rem(slot, n_proc)
    first_seq = jnp.where(is_mid, lane * n_mid, n_proc * n_mid + lane * n_out)
    partner = (1 - half) * half_devs + lax.rem(slot + n_proc, half_devs)

    def frame_peer(step):
        return lax.rem(me_f + step, n_frame)

    def time_slot(owner):
        if span == rows:
            return pl.ds(owner * heads_dev, heads_dev), pl.ds(0, span)
        cuts = rows // span
        return (
            pl.ds(owner // cuts, 1),
            pl.ds(pl.multiple_of(lax.rem(owner, cuts) * span, span), span),
        )

    def send(src, dst, send_sem, recv_sem, where):
        pltpu.make_async_remote_copy(
            src_ref=src,
            dst_ref=dst,
            send_sem=send_sem,
            recv_sem=recv_sem,
            device_id=where,
            device_id_type=MESH,
        ).start()

    def wait_bytes(ref, sem):
        pltpu.make_async_copy(ref, ref, sem).wait()

    barrier = pltpu.get_barrier_semaphore()
    for step in range(1, n_patch):
        peer = lax.rem(me_p + step, n_patch)
        pl.semaphore_signal(barrier, inc=1, device_id={"patch": peer}, device_id_type=MESH)
    for step in range(1, n_frame):
        pl.semaphore_signal(barrier, inc=1, device_id={"frame": frame_peer(step)}, device_id_type=MESH)
    pl.semaphore_wait(barrier, n_patch + n_frame - 2)

    my_rows = pl.ds(pl.multiple_of(slot * rows, rows), rows)
    place = (0, 2, 3, 1)

    def send_rows(owner, seq, c):
        for a in range(4):
            source = space_in[a].at[seq]
            target = sp.at[c, place[a], my_rows]

            @pl.when(owner != slot)
            def _():
                send(source, target, sp_send.at[a], sp_recv.at[c], {"patch": half * half_devs + owner})

            @pl.when(owner == slot)
            def _():
                pltpu.make_async_copy(source, target, sp_recv.at[c]).start()

    def send_space(c):
        for j in range(n_proc):
            send_rows(mid_slot + j, j * n_mid + c, c)

        @pl.when(lax.rem(c, ratio) == 0)
        def _():
            for j in range(n_proc):
                send_rows(out_slot + j, n_proc * n_mid + j * n_out + c // ratio, c // ratio)

    def send_time(c):
        here = pl.ds(c, 1)
        there = pl.ds(me_f * frames + c, 1)
        for step in range(1, n_frame):
            peer = frame_peer(step)
            hs, ps = time_slot(peer)
            for a in range(4):
                send(
                    time_in[a].at[here, hs, ps], tm.at[a, there], tm_send.at[0], tm_recv.at[0], {"frame": peer}
                )
        hs, ps = time_slot(me_f)
        for a in range(4):
            pltpu.make_async_copy(time_in[a].at[here, hs, ps], tm.at[a, there], tm_recv.at[0]).start()

    ahead = min(6, n_mid)

    @pl.loop(0, ahead)
    def _(c):
        send_space(c)

    units = span // ROWS
    total = n_frame * frames
    time_units = heads_dev * units

    def time_unit(u):
        hh = u // units
        ps = pl.ds(pl.multiple_of(lax.rem(u, units) * ROWS, ROWS), ROWS)

        def load(a, start, count):
            block = tm[a, pl.ds(start // ROWS, count // ROWS), hh, ps, :]
            return block.reshape(count, block.shape[-1])

        def store(a, start, value):
            count = value.shape[0]
            tm_res[a, pl.ds(start // ROWS, count // ROWS), hh, ps, :] = value.reshape(
                count // ROWS, ROWS, value.shape[1]
            )

        attend(total * ROWS, scale, ROWS, load, store, dk_acc, dv_acc)

    def return_time(hh):
        if span == rows:
            hs, ps = pl.ds(me_f * heads_dev + hh, 1), pl.ds(0, span)
        else:
            hs, ps = time_slot(me_f)
        head = pl.ds(hh, 1)
        for step in range(1, n_frame):
            peer = frame_peer(step)
            for a in range(3):
                send(
                    tm_res.at[a, pl.ds(peer * frames, frames), head],
                    time_out[a].at[:, hs, ps],
                    tmb_send.at[0],
                    tmb_recv.at[a],
                    {"frame": peer},
                )
        for a in range(3):
            pltpu.make_async_copy(
                tm_res.at[a, pl.ds(me_f * frames, frames), head], time_out[a].at[:, hs, ps], tmb_recv.at[a]
            ).start()

    def relay(k):
        wait_bytes(sp.at[k], sp_recv.at[k])
        send(sp.at[k, pl.ds(0, 2)], xp.at[k], xp_send.at[0], xp_recv.at[k], {"patch": partner})

    def sides(k):
        return ((sp[k, 0], sp[k, 1]), (xp[k, 0], xp[k, 1]))

    def first_pass(k):
        wait_bytes(xp.at[k], xp_recv.at[k])
        at = lax.rem(k, ring)
        for side, (query, upstream) in enumerate(sides(k)):
            raised, grad_prob, top, mass, drift = half_scores(sp[k, 2], sp[k, 3], query, upstream, scale)
            e_ring[at, side] = raised
            p_ring[at, side] = grad_prob
            st_out[k, side] = jnp.broadcast_to(top, (8, half_rows))
            st_out[k, side, pl.ds(1, 1), :] = mass
            st_out[k, side, pl.ds(2, 1), :] = drift
        send(st_out.at[k], st_in.at[k], st_send.at[0], st_recv.at[k], {"patch": partner})

    def give(k, a):
        seq = first_seq + k
        for step in range(1, half_devs):
            other = lax.rem(slot + step, half_devs)
            send(
                res.at[k, a, pl.ds(pl.multiple_of(other * rows, rows), rows)],
                space_out[a].at[seq],
                res_send.at[a],
                res_recv.at[a],
                {"patch": half * half_devs + other},
            )
        pltpu.make_async_copy(res.at[k, a, my_rows], space_out[a].at[seq], res_recv.at[a]).start()

    def second_pass(k):
        wait_bytes(st_in.at[k], st_recv.at[k])
        at = lax.rem(k, ring)
        keys = sp[k, 2]
        dk = dv = None
        for side, (query, upstream) in enumerate(sides(k)):
            mine, theirs = st_out[k, side], st_in[k, 1 - side]
            top = jnp.maximum(mine[0:1], theirs[0:1])
            my_part, their_part = jnp.exp(mine[0:1] - top), jnp.exp(theirs[0:1] - top)
            inverse = 1.0 / (mine[1:2] * my_part + theirs[1:2] * their_part)
            delta = (mine[2:3] * my_part + theirs[2:3] * their_part) * inverse
            soft = e_ring[at, side] * (my_part * inverse)
            weights = soft.astype(jnp.bfloat16)
            grad_score = (soft * (p_ring[at, side] - delta)).astype(jnp.bfloat16)
            dv_side = jnp.dot(weights, upstream, preferred_element_type=jnp.float32)
            dk_side = jnp.dot(grad_score, query, preferred_element_type=jnp.float32)
            dk = dk_side if dk is None else dk + dk_side
            dv = dv_side if dv is None else dv + dv_side
            dq = lead_dot(grad_score, keys) * scale
            if side == 0:
                dq_own[at] = dq
            else:
                dq_out[k] = dq.astype(jnp.bfloat16)
        send(dq_out.at[k], dq_in.at[k], dq_send.at[0], dq_recv.at[k], {"patch": partner})
        res[k, 1] = (dk * scale).astype(jnp.bfloat16)
        res[k, 2] = dv.astype(jnp.bfloat16)
        give(k, 1)
        give(k, 2)

    def finish(k):
        wait_bytes(dq_in.at[k], dq_recv.at[k])
        res[k, 0] = (dq_own[lax.rem(k, ring)] + dq_in[k].astype(jnp.float32)).astype(jnp.bfloat16)
        give(k, 0)

    time_start = frames
    pace = 2
    steps = max(n_mid + 3 * lag, (n_out + 3) * ratio, time_start + pace * time_units)

    @pl.loop(0, steps)
    def _(t):
        for stage, work in enumerate((relay, first_pass, second_pass, finish)):
            k_mid = t - stage * lag
            k_out = t // ratio - stage
            go_mid = jnp.logical_and(is_mid, jnp.logical_and(k_mid >= 0, k_mid < n_mid))
            go_out = jnp.logical_and(
                jnp.logical_and(jnp.logical_not(is_mid), lax.rem(t, ratio) == 0),
                jnp.logical_and(k_out >= 0, k_out < n_out),
            )

            @pl.when(jnp.logical_or(go_mid, go_out))
            def _():
                work(jnp.where(is_mid, k_mid, k_out))

            if stage == 0:

                @pl.when(t < n_mid - ahead)
                def _():
                    send_space(t + ahead)

                @pl.when(t < frames)
                def _():
                    send_time(t)

        @pl.when(t == time_start)
        def _():
            wait_bytes(tm, tm_recv.at[0])

        u = (t - time_start) // pace

        @pl.when(
            jnp.logical_and(
                jnp.logical_and(t >= time_start, lax.rem(t, pace) == time_start % pace), u < time_units
            )
        )
        def _():
            time_unit(u)

            @pl.when(lax.rem(u, units) == units - 1)
            def _():
                return_time(u // units)

    def settle(count):
        part = pl.ds(0, count)
        for a in range(4):
            wait_bytes(space_in[a].at[pl.ds(0, n_seq - count)], sp_send.at[a])
        wait_bytes(xp.at[part], xp_send.at[0])
        wait_bytes(st_in.at[part], st_send.at[0])
        wait_bytes(dq_in.at[part], dq_send.at[0])
        for a in range(3):
            wait_bytes(res.at[part, a, pl.ds(0, half_rows - rows)], res_send.at[a])

    @pl.when(is_mid)
    def _():
        settle(n_mid)

    @pl.when(jnp.logical_not(is_mid))
    def _():
        settle(n_out)

    away = pl.ds(0, (n_frame - 1) * frames)
    wait_bytes(tm.at[:, away], tm_send.at[0])
    wait_bytes(tm_res.at[:, away], tmb_send.at[0])
    for a in range(3):
        wait_bytes(time_out[a], tmb_recv.at[a])
        wait_bytes(space_out[a], res_recv.at[a])


def copy_out(*refs):
    sources, targets, sems = refs[:6], refs[6:12], refs[12]
    copies = [
        pltpu.make_async_copy(source, target, sems.at[i])
        for i, (source, target) in enumerate(zip(sources, targets))
    ]
    for copy in copies:
        copy.start()
    for copy in copies:
        copy.wait()


def per_device(n_frame, n_patch, *blocks):
    frames, heads, rows, dim = blocks[0].shape
    n_seq = frames * heads
    n_pair = n_seq // (n_patch // 4)
    n_mid = n_pair - n_pair // 4
    half_rows = n_patch // 2 * rows
    lag = 3 if half_rows <= 256 else 1
    if n_frame <= heads:
        heads_dev, span = heads // n_frame, rows
    else:
        heads_dev, span = 1, rows * heads // n_frame
    total = n_frame * frames
    scale = 1.0 / math.sqrt(dim)
    plan = (n_patch, n_frame, n_seq, rows, frames, heads_dev, span, lag, scale)
    longest = total * ROWS
    f32 = jnp.float32
    flat = (frames * heads, rows, dim)
    whole = (frames, heads, rows, dim)
    bf16 = jnp.bfloat16
    hbm = pl.BlockSpec(memory_space=pltpu.HBM)
    vmem = pl.BlockSpec(memory_space=pltpu.VMEM)
    dma = pltpu.SemaphoreType.DMA
    sent = [b.reshape(flat) for b in blocks[:4]] + list(blocks[4:])
    outs = pl.pallas_call(
        functools.partial(kernel, plan),
        out_shape=[pltpu.VMEM(flat, bf16)] * 3 + [pltpu.VMEM(whole, bf16)] * 3,
        in_specs=[hbm] * 8,
        out_specs=[vmem] * 6,
        scratch_shapes=[
            pltpu.VMEM((n_mid, 4, half_rows, dim), bf16),
            pltpu.VMEM((n_mid, 2, half_rows, dim), bf16),
            pltpu.VMEM((n_mid, 3, half_rows, dim), bf16),
            pltpu.VMEM((n_mid, half_rows, dim), bf16),
            pltpu.VMEM((n_mid, half_rows, dim), bf16),
            pltpu.VMEM((lag + 1, half_rows, dim), f32),
            pltpu.VMEM((n_mid, 2, 8, half_rows), f32),
            pltpu.VMEM((n_mid, 2, 8, half_rows), f32),
            pltpu.VMEM((lag + 1, 2, half_rows, half_rows), f32),
            pltpu.VMEM((lag + 1, 2, half_rows, half_rows), f32),
            pltpu.VMEM((4, total, heads_dev, span, dim), bf16),
            pltpu.VMEM((3, total, heads_dev, span, dim), bf16),
            pltpu.VMEM((longest, dim), f32),
            pltpu.VMEM((longest, dim), f32),
            dma((n_mid,)),
            dma((4,)),
            dma((n_mid,)),
            dma((1,)),
            dma((n_mid,)),
            dma((1,)),
            dma((n_mid,)),
            dma((1,)),
            dma((3,)),
            dma((3,)),
            dma((1,)),
            dma((1,)),
            dma((3,)),
            dma((1,)),
        ],
        compiler_params=pltpu.CompilerParams(
            collective_id=0, has_side_effects=True, vmem_limit_bytes=52 * 1024 * 1024
        ),
    )(*[pltpu.with_memory_space_constraint(b, pltpu.HBM) for b in sent])
    return pl.pallas_call(
        copy_out,
        out_shape=[jax.ShapeDtypeStruct(whole, bf16)] * 6,
        in_specs=[vmem] * 6,
        out_specs=[hbm] * 6,
        scratch_shapes=[dma((6,))],
        compiler_params=pltpu.CompilerParams(vmem_limit_bytes=1024 * 1024),
    )(*[o.reshape(whole) for o in outs])


def solution(mesh):
    spec = P("frame", None, "patch", None)
    return jax.shard_map(
        functools.partial(per_device, mesh.shape["frame"], mesh.shape["patch"]),
        mesh=mesh,
        in_specs=(spec,) * 8,
        out_specs=(spec,) * 6,
        check_vma=False,
    )
```

```python
import functools
import math

import jax
import jax.numpy as jnp
from jax import lax
from jax.experimental import pallas as pl
from jax.experimental.pallas import tpu as pltpu
from jax.sharding import PartitionSpec as P

MESH = pl.DeviceIdType.MESH
ROWS = 16
BLOCK = 256


def flip_dot(left, right):
    return lax.dot_general(
        left, right, (((1,), (1,)), ((), ())), preferred_element_type=jnp.float32
    )


def lead_dot(left, right):
    return lax.dot_general(
        left, right, (((0,), (0,)), ((), ())), preferred_element_type=jnp.float32
    )


def attend(length, scale, group, load, store, dk_acc, dv_acc):
    for start in range(0, length, BLOCK):
        rows = min(BLOCK, length - start)
        seen = start + rows if group else length
        query = load(0, start, rows)
        keys = load(1, 0, seen)
        values = load(2, 0, seen)
        upstream = load(3, start, rows)
        scores = flip_dot(keys, query) * scale
        if group:
            gap = (
                lax.broadcasted_iota(jnp.int32, (seen, rows), 1)
                + start
                - lax.broadcasted_iota(jnp.int32, (seen, rows), 0)
            )
            allowed = jnp.logical_and(gap >= 0, (gap & (group - 1)) == 0)
            scores = jnp.where(allowed, scores, -1e30)
        raised = jnp.exp(scores - jnp.max(scores, axis=0, keepdims=True))
        soft = raised * (1.0 / jnp.sum(raised, axis=0, keepdims=True))
        weights = soft.astype(jnp.bfloat16)
        grad_prob = flip_dot(values, upstream)
        delta = jnp.sum(weights.astype(jnp.float32) * grad_prob, axis=0, keepdims=True)
        grad_score = (soft * (grad_prob - delta)).astype(jnp.bfloat16)
        dv = jnp.dot(weights, upstream, preferred_element_type=jnp.float32)
        dk = jnp.dot(grad_score, query, preferred_element_type=jnp.float32)
        store(0, start, (lead_dot(grad_score, keys) * scale).astype(jnp.bfloat16))
        if start == 0 and seen < length:
            dk_acc[pl.ds(seen, length - seen), :] = jnp.zeros((length - seen, dk.shape[1]), jnp.float32)
            dv_acc[pl.ds(seen, length - seen), :] = jnp.zeros((length - seen, dv.shape[1]), jnp.float32)
        if start == 0:
            dk_acc[pl.ds(0, seen), :] = dk
            dv_acc[pl.ds(0, seen), :] = dv
        else:
            dk_acc[pl.ds(0, seen), :] += dk
            dv_acc[pl.ds(0, seen), :] += dv
    store(1, 0, (dk_acc[pl.ds(0, length), :] * scale).astype(jnp.bfloat16))
    store(2, 0, dv_acc[pl.ds(0, length), :].astype(jnp.bfloat16))


def kernel(plan, *refs):
    space_in, time_in = refs[0:4], refs[4:8]
    space_out, time_out = refs[8:11], refs[11:14]
    (sp, sp_res, tm, tm_res, dk_acc, dv_acc) = refs[14:20]
    (sp_recv, sp_send, spb_recv, spb_send, tm_recv, tm_send, tmb_recv, tmb_send) = refs[20:]
    n_patch, n_frame, per_dev, rows, frames, heads_dev, span, scale = plan
    length = n_patch * rows
    me_p = lax.axis_index("patch")
    me_f = lax.axis_index("frame")

    def patch_peer(step):
        return lax.rem(me_p + step, n_patch)

    def frame_peer(step):
        return lax.rem(me_f + step, n_frame)

    def time_slot(owner):
        if span == rows:
            return pl.ds(owner * heads_dev, heads_dev), pl.ds(0, span)
        cuts = rows // span
        return (
            pl.ds(owner // cuts, 1),
            pl.ds(pl.multiple_of(lax.rem(owner, cuts) * span, span), span),
        )

    barrier = pltpu.get_barrier_semaphore()
    for step in range(1, n_patch):
        pl.semaphore_signal(barrier, inc=1, device_id={"patch": patch_peer(step)}, device_id_type=MESH)
    for step in range(1, n_frame):
        pl.semaphore_signal(barrier, inc=1, device_id={"frame": frame_peer(step)}, device_id_type=MESH)
    pl.semaphore_wait(barrier, n_patch + n_frame - 2)

    my_rows = pl.ds(pl.multiple_of(me_p * rows, rows), rows)
    pieces = max(1, per_dev // 2)
    piece_frames = frames // pieces

    def send_space(c):
        for step in range(1, n_patch):
            peer = patch_peer(step)
            for a in range(4):
                pltpu.make_async_remote_copy(
                    src_ref=space_in[a].at[peer * per_dev + c],
                    dst_ref=sp.at[c, a, my_rows],
                    send_sem=sp_send.at[c],
                    recv_sem=sp_recv.at[c],
                    device_id={"patch": peer},
                    device_id_type=MESH,
                ).start()
        for a in range(4):
            pltpu.make_async_copy(
                space_in[a].at[me_p * per_dev + c], sp.at[c, a, my_rows], sp_recv.at[c]
            ).start()

    def send_time(c):
        here = pl.ds(c * piece_frames, piece_frames)
        there = pl.ds(me_f * frames + c * piece_frames, piece_frames)
        for step in range(1, n_frame):
            peer = frame_peer(step)
            hs, ps = time_slot(peer)
            for a in range(4):
                pltpu.make_async_remote_copy(
                    src_ref=time_in[a].at[here, hs, ps],
                    dst_ref=tm.at[a, there],
                    send_sem=tm_send.at[0],
                    recv_sem=tm_recv.at[0],
                    device_id={"frame": peer},
                    device_id_type=MESH,
                ).start()
        hs, ps = time_slot(me_f)
        for a in range(4):
            pltpu.make_async_copy(time_in[a].at[here, hs, ps], tm.at[a, there], tm_recv.at[0]).start()

    @pl.loop(0, pieces)
    def _(c):
        send_space(c)
        send_time(c)

    @pl.loop(pieces, per_dev)
    def _(c):
        send_space(c)

    def all_time():
        pltpu.make_async_copy(tm, tm, tm_recv.at[0]).wait()
        units = span // ROWS
        total = n_frame * frames

        @pl.loop(0, heads_dev * units)
        def _(u):
            hh = u // units
            ps = pl.ds(pl.multiple_of(lax.rem(u, units) * ROWS, ROWS), ROWS)

            def load(a, start, count):
                block = tm[a, pl.ds(start // ROWS, count // ROWS), hh, ps, :]
                return block.reshape(count, block.shape[-1])

            def store(a, start, value):
                count = value.shape[0]
                tm_res[a, pl.ds(start // ROWS, count // ROWS), hh, ps, :] = value.reshape(
                    count // ROWS, ROWS, value.shape[1]
                )

            attend(total * ROWS, scale, ROWS, load, store, dk_acc, dv_acc)

        hs, ps = time_slot(me_f)
        for step in range(1, n_frame):
            peer = frame_peer(step)
            for a in range(3):
                pltpu.make_async_remote_copy(
                    src_ref=tm_res.at[a, pl.ds(peer * frames, frames)],
                    dst_ref=time_out[a].at[:, hs, ps],
                    send_sem=tmb_send.at[0],
                    recv_sem=tmb_recv.at[a],
                    device_id={"frame": peer},
                    device_id_type=MESH,
                ).start()
        for a in range(3):
            pltpu.make_async_copy(
                tm_res.at[a, pl.ds(me_f * frames, frames)], time_out[a].at[:, hs, ps], tmb_recv.at[a]
            ).start()

    @pl.loop(0, per_dev)
    def _(c):
        @pl.when(c == pieces)
        def _():
            all_time()

        pltpu.make_async_copy(sp.at[c], sp.at[c], sp_recv.at[c]).wait()

        def load(a, start, count):
            return sp[c, a, pl.ds(start, count), :]

        def store(a, start, value):
            sp_res[c, a, pl.ds(start, value.shape[0]), :] = value

        attend(length, scale, 0, load, store, dk_acc, dv_acc)
        seq = me_p * per_dev + c
        for step in range(1, n_patch):
            peer = patch_peer(step)
            for a in range(3):
                pltpu.make_async_remote_copy(
                    src_ref=sp_res.at[c, a, pl.ds(pl.multiple_of(peer * rows, rows), rows)],
                    dst_ref=space_out[a].at[seq],
                    send_sem=spb_send.at[c],
                    recv_sem=spb_recv.at[a],
                    device_id={"patch": peer},
                    device_id_type=MESH,
                ).start()
        for a in range(3):
            pltpu.make_async_copy(sp_res.at[c, a, my_rows], space_out[a].at[seq], spb_recv.at[a]).start()

    others = pl.ds(0, length - rows)
    away = pl.ds(0, (n_frame - 1) * frames)

    @pl.loop(0, per_dev)
    def _(c):
        pltpu.make_async_copy(sp.at[c, :, others], sp.at[c, :, others], sp_send.at[c]).wait()
        pltpu.make_async_copy(sp_res.at[c, :, others], sp_res.at[c, :, others], spb_send.at[c]).wait()

    pltpu.make_async_copy(tm.at[:, away], tm.at[:, away], tm_send.at[0]).wait()
    pltpu.make_async_copy(tm_res.at[:, away], tm_res.at[:, away], tmb_send.at[0]).wait()
    for a in range(3):
        pltpu.make_async_copy(time_out[a], time_out[a], tmb_recv.at[a]).wait()
        pltpu.make_async_copy(space_out[a], space_out[a], spb_recv.at[a]).wait()


def copy_out(*refs):
    sources, targets, sems = refs[:6], refs[6:12], refs[12]
    copies = [
        pltpu.make_async_copy(source, target, sems.at[i])
        for i, (source, target) in enumerate(zip(sources, targets))
    ]
    for copy in copies:
        copy.start()
    for copy in copies:
        copy.wait()


def per_device(n_frame, n_patch, *blocks):
    frames, heads, rows, dim = blocks[0].shape
    per_dev = frames * heads // n_patch
    if n_frame <= heads:
        heads_dev, span = heads // n_frame, rows
    else:
        heads_dev, span = 1, rows * heads // n_frame
    length = n_patch * rows
    total = n_frame * frames
    scale = 1.0 / math.sqrt(dim)
    plan = (n_patch, n_frame, per_dev, rows, frames, heads_dev, span, scale)
    longest = max(length, total * ROWS)
    flat = (frames * heads, rows, dim)
    whole = (frames, heads, rows, dim)
    bf16 = jnp.bfloat16
    hbm = pl.BlockSpec(memory_space=pltpu.HBM)
    vmem = pl.BlockSpec(memory_space=pltpu.VMEM)
    dma = pltpu.SemaphoreType.DMA
    sent = [b.reshape(flat) for b in blocks[:4]] + list(blocks[4:])
    outs = pl.pallas_call(
        functools.partial(kernel, plan),
        out_shape=[pltpu.VMEM(flat, bf16)] * 3 + [pltpu.VMEM(whole, bf16)] * 3,
        in_specs=[hbm] * 8,
        out_specs=[vmem] * 6,
        scratch_shapes=[
            pltpu.VMEM((per_dev, 4, length, dim), bf16),
            pltpu.VMEM((per_dev, 3, length, dim), bf16),
            pltpu.VMEM((4, total, heads_dev, span, dim), bf16),
            pltpu.VMEM((3, total, heads_dev, span, dim), bf16),
            pltpu.VMEM((longest, dim), jnp.float32),
            pltpu.VMEM((longest, dim), jnp.float32),
            dma((per_dev,)),
            dma((per_dev,)),
            dma((3,)),
            dma((per_dev,)),
            dma((1,)),
            dma((1,)),
            dma((3,)),
            dma((1,)),
        ],
        compiler_params=pltpu.CompilerParams(
            collective_id=0, has_side_effects=True, vmem_limit_bytes=40 * 1024 * 1024
        ),
    )(*[pltpu.with_memory_space_constraint(b, pltpu.HBM) for b in sent])
    return pl.pallas_call(
        copy_out,
        out_shape=[jax.ShapeDtypeStruct(whole, bf16)] * 6,
        in_specs=[vmem] * 6,
        out_specs=[hbm] * 6,
        scratch_shapes=[dma((6,))],
        compiler_params=pltpu.CompilerParams(vmem_limit_bytes=1024 * 1024),
    )(*[o.reshape(whole) for o in outs])


def solution(mesh):
    spec = P("frame", None, "patch", None)
    return jax.shard_map(
        functools.partial(per_device, mesh.shape["frame"], mesh.shape["patch"]),
        mesh=mesh,
        in_specs=(spec,) * 8,
        out_specs=(spec,) * 6,
        check_vma=False,
    )
```
